32 devices in a mesh: groups: 2 (over y), replica: 8 (over z, x), tensor: 2 (over core).
Axes of the slice: x: 2, y: 2, z: 4, core: 2. Of those that a mesh axis runs over, the one named last changes fastest.
Arguments:
- hidden_states: bfloat16 [16384, 8192], P(('groups', 'replica'), 'tensor'), parts along dimension 0, may hold values from -6 to 6
- kv_weight: bfloat16 [8192, 2, 1024], P('tensor'), may hold values from -0.0625 to 0.0625
- pool_down: bfloat16 [32, 8192, 2, 128], P(('groups', 'replica'), 'tensor'), parts along dimension 0, may hold values from -0.0625 to 0.0625
- pool_up: bfloat16 [32, 2, 128, 1024], P(('groups', 'replica'), None, None, 'tensor'), parts along dimension 0, may hold values from -3 to 3
- adapter_rank: int32 [32], P('groups'), parts along dimension 0, may hold values from 16 to 128, as said below
- pool_row: int32 [32], P('groups'), parts along dimension 0, may hold values from 0 to 15, as said below
- request_adapter: int32 [16, 8], P(('groups', 'replica')), parts along dimension 0, may hold values from 0 to 15, as said below
- request_length: int32 [16, 8], P(('groups', 'replica')), parts along dimension 0, may hold values from 1 to 512, 1024 in all within a row
Outputs:
- keys: bfloat16 [16384, 1024], P(('groups', 'replica'), 'tensor'), parts along dimension 0
- values: bfloat16 [16384, 1024], P(('groups', 'replica'), 'tensor'), parts along dimension 0
The draws below stay inside these ranges and needn't reach their ends.
There are 2 independent parts, one for each index of `groups`. The reference program is written for one: setup_inputs(seed, part) draws one part's arguments, and reference() takes and returns one part's arrays. A program takes and returns all parts, laid end to end along the dimension named above; an argument that names none is the same for every part. Nothing has to cross between parts.
Inputs may be any that keep to these rules, and one draw needn't show every extreme that they name: `pool_row`: a permutation: every pool row holds one adapter. `adapter_rank`: each of 16, 32, 64 and 128; some adapter has rank 128. `request_adapter`: at most 1 request of one replica index name adapters held in the pool rows of any one replica index (rows q * 2 to (q+1) * 2 - 1 belong to index q), and some replica index reaches 1 from some index.
All inputs are finite; a program needn't handle non-finite values.
Results may differ from the reference program's by a relative error of at most 0.0095.
Values may be sent and summed in bfloat16 or wider, within the bound.
No kernel may reach another device: no remote copies, remote signals or barrier semaphores. Data moves between devices by JAX's collectives and lax.ppermute only.
A program may use at most 256 MiB of HBM per device.

```python
import math
import jax
import jax.numpy as jnp
import numpy as np
from jax import lax

D = 8192
KVW = 1024
RMAX = 128
TOK_DEV = 1024
REQ_DEV = 8
ADP_DEV = 2
LMAX = 512
TOKENS = 8192
ADAPTERS = 16
CAP = 1
N_REPLICA = 8
N_TENSOR = 2


def pool_layout(key):
    shuffle = jax.random.permutation(jax.random.fold_in(key, 11), ADAPTERS).astype(jnp.int32)
    holder = jnp.argsort(shuffle).astype(jnp.int32)
    device_keys = jax.random.split(jax.random.fold_in(key, 12), N_REPLICA)
    places = jax.vmap(lambda k: jax.random.permutation(k, N_REPLICA * CAP)[:REQ_DEV])(device_keys).astype(jnp.int32)
    owners = places % N_REPLICA
    slots = jax.random.randint(jax.random.fold_in(key, 13), (N_REPLICA, REQ_DEV), 0, ADP_DEV).astype(jnp.int32)
    chosen = holder[owners * ADP_DEV + slots]
    return (shuffle, chosen)


def draw_pool_row(key, part):
    shuffle, chosen = pool_layout(key)
    return shuffle


def draw_request_adapter(key, part):
    shuffle, chosen = pool_layout(key)
    return chosen


def draw_adapter_rank(key, part):
    key = jax.random.fold_in(key, 3)
    powers = jax.random.randint(key, (ADAPTERS,), 0, 4)
    ranks = RMAX // 8 * jnp.power(2, powers).astype(jnp.int32)
    chosen = jax.random.randint(jax.random.fold_in(key, 5), (), 0, ADAPTERS)
    return jnp.where(jnp.arange(ADAPTERS) == chosen, RMAX, ranks).astype(jnp.int32)


def block_scale(key, extent, cuts, low, top_value):
    gain = 1.0
    for dim, blocks in cuts:
        steps = jax.random.uniform(jax.random.fold_in(jax.random.fold_in(key, 6), dim), (blocks,), jnp.float32, low / len(cuts), top_value / len(cuts))
        gain = gain * jnp.repeat(jnp.exp(steps), extent[dim] // blocks).reshape((-1,) + (1,) * (len(extent) - 1 - dim))
    return gain


def length_profile(amount, total, limit, lean):
    loads = [(1 << 20) // math.isqrt(grade ** lean) + 1 for grade in range(2, amount + 1)]
    surplus, given = total - limit - (amount - 1), [1] * (amount - 1)
    while surplus > 0:
        movable = [i for i in range(amount - 1) if given[i] < limit]
        pool, remaining = sum([loads[i] for i in movable]), surplus
        for i in movable:
            addition = min(limit - given[i], max(1, remaining * loads[i] // pool), surplus)
            given[i] = given[i] + addition
            surplus = surplus - addition
    return np.array([limit] + given)


def ragged_sizes(own_key, number_of, total, most, skew):
    if number_of == 2:
        one = jax.random.randint(own_key, (), max(1, total - most), min(most, total - 1) + 1)
        return jnp.stack([one, total - one])
    tallies = jnp.asarray(length_profile(number_of, total, most, skew), jnp.int32)
    twos = (number_of - 1) // 2
    giver, taker = tallies[1:1 + 2 * twos:2], tallies[2:2 + 2 * twos:2]
    margin = jnp.minimum(giver - 1, most - taker)
    passed = jax.random.randint(jax.random.fold_in(own_key, 1), (twos,), 0, 1 << 20) % (margin + 1)
    tallies = tallies.at[1:1 + 2 * twos:2].set(giver - passed).at[2:2 + 2 * twos:2].set(taker + passed)
    return tallies[jax.random.permutation(jax.random.fold_in(own_key, 2), number_of)]


def bell_draw(rng, dims, width, most, cuts=(), kind=jnp.bfloat16):
    gain = block_scale(rng, dims, cuts, -0.22, 0.18) if cuts else 1.0
    array = jax.random.normal(rng, dims, jnp.float32) * width * gain
    return jnp.minimum(jnp.maximum(array, -most), most).astype(kind)


def setup_inputs(seed: int = 0, part: int = 0) -> dict:
    key_list = jax.random.split(jax.random.key(seed), 9)
    own_keys = jax.random.split(jax.random.fold_in(key_list[8], part), 9)
    return {
        "hidden_states": bell_draw(own_keys[0], (TOKENS, D), 1.0, 6.0, ((0, 8), (1, 2))),
        "kv_weight": bell_draw(key_list[1], (D, 2, KVW), D ** -0.5, 0.0625, ((0, 2),)),
        "pool_down": bell_draw(own_keys[2], (ADAPTERS, D, 2, RMAX), D ** -0.5, 0.0625, ((0, 8), (1, 2))),
        "pool_up": bell_draw(own_keys[3], (ADAPTERS, 2, RMAX, KVW), 0.5, 3.0, ((0, 8), (3, 2))),
        "adapter_rank": draw_adapter_rank(jax.random.fold_in(jax.random.fold_in(key_list[8], part), 71), part),
        "pool_row": draw_pool_row(jax.random.fold_in(jax.random.fold_in(key_list[8], part), 71), part),
        "request_adapter": draw_request_adapter(jax.random.fold_in(jax.random.fold_in(key_list[8], part), 71), part),
        "request_length": jax.vmap(lambda own: ragged_sizes(own, REQ_DEV, TOK_DEV, LMAX, 2))(jax.random.split(own_keys[7], N_REPLICA)).reshape((N_REPLICA, REQ_DEV)).astype(jnp.int32),
    }


def reference(hidden_states, kv_weight, pool_down, pool_up, adapter_rank, pool_row, request_adapter, request_length):
    width_dev = D // N_TENSOR
    base = jnp.zeros((TOKENS, 2 * KVW), jnp.float32)
    for t in range(N_TENSOR):
        term = jnp.dot(hidden_states[:, t * width_dev:(t + 1) * width_dev], kv_weight[t * width_dev:(t + 1) * width_dev].reshape(width_dev, 2 * KVW), preferred_element_type=jnp.float32)
        base = base + lax.optimization_barrier(term.astype(jnp.bfloat16)).astype(jnp.float32)
    lengths = request_length.astype(jnp.int32)
    within = jnp.cumsum(lengths, axis=1) - lengths
    starts = (within + (jnp.arange(N_REPLICA, dtype=jnp.int32) * TOK_DEV)[:, None]).reshape(-1).astype(jnp.int32)
    flat_len = lengths.reshape(-1)
    adapters = request_adapter.reshape(-1)
    rows_of = pool_row[adapters].astype(jnp.int32)
    ranks = adapter_rank[adapters].astype(jnp.int32)
    padded = jnp.concatenate([hidden_states, jnp.zeros((LMAX, D), hidden_states.dtype)], axis=0)
    column = jnp.arange(RMAX, dtype=jnp.int32)
    position = jnp.arange(LMAX, dtype=jnp.int32)

    def one_request(i, delta):
        start = starts[i]
        block = lax.dynamic_slice_in_dim(padded, start, LMAX, 0)
        down = lax.dynamic_index_in_dim(pool_down, rows_of[i], 0, keepdims=False)
        shrink = jnp.dot(block, down.reshape(D, 2 * RMAX), preferred_element_type=jnp.float32).reshape(LMAX, 2, RMAX)
        factor = jnp.where(column < ranks[i], 1.0 / jnp.sqrt(ranks[i].astype(jnp.float32)), 0.0).astype(jnp.float32)
        live = position < flat_len[i]
        shrink = jnp.where(live[:, None, None], shrink * factor[None, None, :], 0.0).astype(jnp.bfloat16)
        upper = lax.dynamic_index_in_dim(pool_up, rows_of[i], 0, keepdims=False)
        grown = jnp.einsum('sar,arc->sac', shrink.astype(jnp.float32), upper.astype(jnp.float32))
        current = lax.dynamic_slice_in_dim(delta, start, LMAX, 0)
        return lax.dynamic_update_slice_in_dim(delta, current + grown.reshape(LMAX, 2 * KVW), start, 0)
    delta = lax.fori_loop(0, N_REPLICA * REQ_DEV, one_request, jnp.zeros((TOKENS + LMAX, 2 * KVW), jnp.float32))
    total = base + delta[:TOKENS]
    return (total[:, :KVW].astype(jnp.bfloat16), total[:, KVW:].astype(jnp.bfloat16))
```

```python
import functools

import jax
import jax.numpy as jnp
from jax import lax
from jax.experimental import pallas as pl
from jax.experimental.pallas import tpu as pltpu
from jax.sharding import PartitionSpec as P

TILE = 128
BF16 = jnp.bfloat16
F32 = jnp.float32


def table_lookup(indices, table):
    hit = indices[:, None] == jnp.arange(table.shape[0], dtype=jnp.int32)[None, :]
    return jnp.sum(jnp.where(hit, table[None, :], 0), axis=1)


def visit_list(lengths, slots, ranks, rows):
    count = lengths.shape[0]
    steps = rows // TILE + count - 1
    ends = jnp.cumsum(lengths)
    starts = ends - lengths
    first = starts // TILE
    tiles = (ends - 1) // TILE - first + 1
    upto = jnp.cumsum(tiles)
    step = jnp.arange(steps, dtype=jnp.int32)
    live = step < upto[-1]
    request = jnp.minimum(jnp.sum((step[:, None] >= upto[None, :]).astype(jnp.int32), axis=1), count - 1)
    pick = lambda t: table_lookup(request, t)
    tile = jnp.where(live, pick(first) + step - pick(upto - tiles), rows // TILE - 1)
    begin = jnp.where(live, pick(starts), 0)
    end = jnp.where(live, pick(ends), 0)
    return tile, pick(slots), begin, end, pick(ranks)


def shrink_kernel(tile, slot, begin, end, rank, scale, h_ref, d_ref, o_ref):
    i = pl.program_id(0)
    top = tile[i] * TILE
    grown = jnp.dot(h_ref[...], d_ref[0], preferred_element_type=F32) * scale[i]
    row = lax.broadcasted_iota(jnp.int32, grown.shape, 0) + top
    col = lax.broadcasted_iota(jnp.int32, grown.shape, 1)
    half = grown.shape[1] // 2
    col = jnp.where(col >= half, col - half, col)
    mine = (row >= begin[i]) & (row < end[i])
    value = jnp.where(col < rank[i], grown, 0.0)
    fresh = jnp.logical_or(i == 0, tile[i] != tile[jnp.maximum(i - 1, 0)])

    @pl.when(fresh)
    def _():
        o_ref[...] = jnp.where(mine, value, 0.0).astype(o_ref.dtype)

    @pl.when(jnp.logical_not(fresh))
    def _():
        o_ref[...] = jnp.where(mine, value, o_ref[...].astype(F32)).astype(o_ref.dtype)


def shrink_call(visits, scale, tokens, downs):
    tile, slot, begin, end, rank = visits
    rows, width = tokens.shape
    cols = downs.shape[2]
    steps = tile.shape[0]
    return pl.pallas_call(
        shrink_kernel,
        grid_spec=pltpu.PrefetchScalarGridSpec(
            num_scalar_prefetch=6,
            grid=(steps,),
            in_specs=[
                pl.BlockSpec((TILE, width), lambda i, t, s, *_: (t[i], 0)),
                pl.BlockSpec((1, width, cols), lambda i, t, s, *_: (s[i], 0, 0)),
            ],
            out_specs=pl.BlockSpec((TILE, cols), lambda i, t, s, *_: (t[i], 0)),
        ),
        out_shape=jax.ShapeDtypeStruct((rows, cols), BF16),
        compiler_params=pltpu.CompilerParams(
            dimension_semantics=("arbitrary",), vmem_limit_bytes=32 * 2**20
        ),
        cost_estimate=pl.CostEstimate(
            flops=2 * steps * TILE * width * cols, bytes_accessed=2 * rows * width * 2, transcendentals=0
        ),
    )(tile, slot, begin, end, rank, scale, tokens, downs)


def grow_kernel(tile, slot, begin, end, rank, s_ref, u_ref, own_ref, other_ref, k_ref, v_ref, acc):
    i = pl.program_id(0)
    steps = pl.num_programs(0)
    top = tile[i] * TILE
    half = s_ref.shape[1] // 2
    feat = k_ref.shape[1]
    row = lax.broadcasted_iota(jnp.int32, (TILE, half), 0) + top
    mine = (row >= begin[i]) & (row < end[i])
    fresh = jnp.logical_or(i == 0, tile[i] != tile[jnp.maximum(i - 1, 0)])

    @pl.when(fresh)
    def _():
        acc[...] = own_ref[...].astype(F32) + other_ref[...].astype(F32)

    for kv in range(2):
        part = s_ref[:, kv * half : (kv + 1) * half]
        part = jnp.where(mine, part.astype(F32), 0.0).astype(BF16)
        cols = slice(kv * feat, (kv + 1) * feat)
        acc[:, cols] += jnp.dot(part, u_ref[0, kv], preferred_element_type=F32)
    last = jnp.logical_or(i == steps - 1, tile[i] != tile[jnp.minimum(i + 1, steps - 1)])

    @pl.when(last)
    def _():
        k_ref[...] = acc[:, :feat].astype(BF16)
        v_ref[...] = acc[:, feat:].astype(BF16)


def grow_call(visits, shrunk, ups, own, other):
    tile, slot, begin, end, rank = visits
    rows, cols = shrunk.shape
    feat = ups.shape[3]
    steps = tile.shape[0]
    by_tile = lambda i, t, *_: (t[i], 0)
    return pl.pallas_call(
        grow_kernel,
        grid_spec=pltpu.PrefetchScalarGridSpec(
            num_scalar_prefetch=5,
            grid=(steps,),
            in_specs=[
                pl.BlockSpec((TILE, cols), by_tile),
                pl.BlockSpec((1,) + ups.shape[1:], lambda i, t, s, *_: (s[i], 0, 0, 0)),
                pl.BlockSpec((TILE, 2 * feat), by_tile),
                pl.BlockSpec((TILE, 2 * feat), by_tile),
            ],
            out_specs=[pl.BlockSpec((TILE, feat), by_tile)] * 2,
            scratch_shapes=[pltpu.VMEM((TILE, 2 * feat), F32)],
        ),
        out_shape=[jax.ShapeDtypeStruct((rows, feat), BF16)] * 2,
        compiler_params=pltpu.CompilerParams(
            dimension_semantics=("arbitrary",), vmem_limit_bytes=32 * 2**20
        ),
        cost_estimate=pl.CostEstimate(
            flops=2 * steps * TILE * cols * feat, bytes_accessed=6 * rows * feat * 2, transcendentals=0
        ),
    )(tile, slot, begin, end, rank, shrunk, ups, own, other)


def per_device(
    replicas,
    cores,
    hidden_states,
    kv_weight,
    pool_down,
    pool_up,
    adapter_rank,
    pool_row,
    request_adapter,
    request_length,
):
    rows, width = hidden_states.shape
    kv_cols = kv_weight.shape[2]
    held, rank_max = pool_down.shape[0], pool_down.shape[3]
    team = 4 if replicas % 4 == 0 else 1
    part = width // team
    me = lax.axis_index("replica")
    core = lax.axis_index("tensor")

    def swap(x, o):
        return lax.ppermute(x, "replica", [(i, i ^ o) for i in range(replicas)])

    def other_core(x):
        return lax.ppermute(x, "tensor", [(0, 1), (1, 0)])

    wanted = table_lookup(request_adapter[0], pool_row)
    table = lax.all_gather(jnp.concatenate([wanted, request_length[0]])[None], "replica", axis=0, tiled=True)
    count = request_length.shape[1]
    place = jnp.arange(pool_row.shape[0], dtype=jnp.int32)
    row_rank = jnp.sum(jnp.where(pool_row[None, :] == place[:, None], adapter_rank[None, :], 0), axis=1)

    def facts(o):
        line = lax.dynamic_slice_in_dim(table, me ^ o, 1, 0)[0]
        return line[:count], line[count:]

    downs = pool_down.reshape(held, width, 2 * rank_max)

    def share(x, axis, o):
        return lax.dynamic_slice_in_dim(x, ((me ^ o) % team) * part, part, axis)

    down_all = [share(downs, 1, 0)] + [swap(share(downs, 1, o), o) for o in range(1, replicas)]
    down_all = jnp.concatenate(down_all, axis=0)
    tokens = [share(hidden_states, 1, 0)] + [swap(share(hidden_states, 1, o), o) for o in range(1, team)]
    tokens = jnp.concatenate(tokens, axis=0)

    product = jnp.dot(
        hidden_states, kv_weight.reshape(width, 2 * kv_cols), preferred_element_type=F32
    ).astype(BF16)
    feat = kv_cols // cores
    if cores == 2:

        def features(c):
            return jnp.concatenate(
                [lax.dynamic_slice_in_dim(product, kv * kv_cols + c * feat, feat, 1) for kv in range(2)], axis=1
            )

        base_own = features(core)
        base_other = other_core(features(1 - core))
    else:
        base_own = jnp.concatenate(
            [
                lax.psum_scatter(
                    product[:, kv * kv_cols : (kv + 1) * kv_cols], "tensor", scatter_dimension=1, tiled=True
                )
                for kv in range(2)
            ],
            axis=1,
        )
        base_other = jnp.zeros_like(base_own)

    def upper(o):
        need, _ = facts(o)
        slot = jnp.sum(jnp.where(need // held == me, need % held, 0))
        return lax.dynamic_slice_in_dim(pool_up, slot, 1, 0)

    ups = jnp.concatenate([upper(0)] + [swap(upper(o), o) for o in range(1, replicas)], axis=0)

    down_all, tokens, ups, base_own, base_other = lax.optimization_barrier(
        (down_all, tokens, ups, base_own, base_other)
    )

    visits = []
    for o in range(team):
        need, lengths = facts(o)
        slots = ((need // held) ^ me) * held + need % held
        ranks = table_lookup(need, row_rank)
        tile, slot, begin, end, rank = visit_list(lengths, slots, ranks, rows)
        visits.append((tile + o * (rows // TILE), slot, begin + o * rows, end + o * rows, rank))
    visits = [jnp.concatenate(v) for v in zip(*visits)]
    scale = 1.0 / jnp.sqrt(visits[4].astype(F32))
    partial = shrink_call(visits, scale, tokens, down_all).reshape(team, rows, 2 * rank_max)
    if cores == 2:
        keep = lax.dynamic_slice_in_dim(partial, core * rank_max, rank_max, 2)
        give = lax.dynamic_slice_in_dim(partial, (1 - core) * rank_max, rank_max, 2)
        partial = (keep.astype(F32) + other_core(give).astype(F32)).astype(BF16)
    else:
        partial = lax.psum(partial, "tensor")
    total = partial[0].astype(F32)
    for o in range(1, team):
        total = total + swap(partial[o], o).astype(F32)
    shrunk = total.astype(BF16)
    if cores == 2:
        peer = other_core(shrunk)
        shrunk = jnp.concatenate(
            [jnp.where(core == 0, shrunk, peer), jnp.where(core == 0, peer, shrunk)], axis=1
        )

    need, lengths = facts(0)
    own_visits = visit_list(lengths, (need // held) ^ me, table_lookup(need, row_rank), rows)
    keys, values = grow_call(own_visits, shrunk, ups, base_own, base_other)
    return keys, values


def solution(mesh):
    placed = (
        P(("groups", "replica"), "tensor"),
        P("tensor", None, None),
        P(("groups", "replica"), "tensor", None, None),
        P(("groups", "replica"), None, None, "tensor"),
        P("groups"),
        P("groups"),
        P(("groups", "replica"), None),
        P(("groups", "replica"), None),
    )
    return jax.shard_map(
        functools.partial(per_device, mesh.shape["replica"], mesh.shape["tensor"]),
        mesh=mesh,
        in_specs=placed,
        out_specs=(P(("groups", "replica"), "tensor"), P(("groups", "replica"), "tensor")),
        check_vma=False,
    )
```

```python
import functools

import jax
import jax.numpy as jnp
from jax import lax
from jax.experimental import pallas as pl
from jax.experimental.pallas import tpu as pltpu
from jax.sharding import PartitionSpec as P

TILE = 256
BF16 = jnp.bfloat16
F32 = jnp.float32


def table_lookup(indices, table):
    hit = indices[:, None] == jnp.arange(table.shape[0], dtype=jnp.int32)[None, :]
    return jnp.sum(jnp.where(hit, table[None, :], 0), axis=1)


def plan(lengths, ranks, rows):
    ends = jnp.cumsum(lengths)
    starts = ends - lengths
    top = jnp.arange(rows // TILE, dtype=jnp.int32) * TILE
    low = jnp.sum((ends[None, :] <= top[:, None]).astype(jnp.int32), axis=1)
    high = jnp.sum((starts[None, :] < top[:, None] + TILE).astype(jnp.int32), axis=1)
    return low, high, starts, ends, ranks, 1.0 / jnp.sqrt(ranks.astype(F32))


def shrink_kernel(tiles, count, low, high, begin, end, rank, scale, slot, h_ref, d_ref, o_ref):
    g = pl.program_id(0)
    top = g % tiles * TILE
    base = g // tiles * count
    shape = o_ref.shape
    half = shape[1] // 2
    o_ref[...] = jnp.zeros(shape, o_ref.dtype)

    @pl.loop(base + low[g], base + high[g])
    def _(j):
        grown = jnp.dot(h_ref[...], d_ref[slot[j]], preferred_element_type=F32) * scale[j]
        row = lax.broadcasted_iota(jnp.int32, shape, 0) + top
        col = lax.broadcasted_iota(jnp.int32, shape, 1)
        col = jnp.where(col >= half, col - half, col)
        mine = (row >= begin[j]) & (row < end[j])
        value = jnp.where(col < rank[j], grown, 0.0)
        o_ref[...] = jnp.where(mine, value, o_ref[...].astype(F32)).astype(o_ref.dtype)


def shrink_call(facts, slot, tokens, downs):
    rows, width = tokens.shape
    cols = downs.shape[2]
    sources, count = slot.shape
    tiles = rows // sources // TILE
    flat = [f.reshape(-1) for f in (*facts, slot)]
    return pl.pallas_call(
        functools.partial(shrink_kernel, tiles, count),
        grid_spec=pltpu.PrefetchScalarGridSpec(
            num_scalar_prefetch=7,
            grid=(sources * tiles,),
            in_specs=[
                pl.BlockSpec((TILE, width), lambda i, *_: (i, 0)),
                pl.BlockSpec(downs.shape, lambda i, *_: (0, 0, 0), pipeline_mode=pl.Buffered(1)),
            ],
            out_specs=pl.BlockSpec((TILE, cols), lambda i, *_: (i, 0)),
        ),
        out_shape=jax.ShapeDtypeStruct((rows, cols), BF16),
        compiler_params=pltpu.CompilerParams(
            dimension_semantics=("arbitrary",), vmem_limit_bytes=24 * 2**20
        ),
        cost_estimate=pl.CostEstimate(
            flops=4 * rows * width * cols, bytes_accessed=2 * rows * width * 2, transcendentals=0
        ),
    )(*flat, tokens, downs)


def grow_kernel(low, high, begin, end, slot, s_ref, u_ref, own_ref, other_ref, k_ref, v_ref):
    g = pl.program_id(0)
    half = s_ref.shape[1] // 2
    outs = (k_ref, v_ref)
    feat = k_ref.shape[1]
    row = lax.broadcasted_iota(jnp.int32, (TILE, feat), 0) + g * TILE
    for kv in range(2):
        cols = slice(kv * feat, (kv + 1) * feat)
        outs[kv][...] = jnp.zeros(k_ref.shape, BF16)

        @pl.loop(low[g], high[g])
        def _(j):
            grown = jnp.dot(s_ref[:, kv * half : (kv + 1) * half], u_ref[slot[j], kv], preferred_element_type=F32)
            grown = grown + (own_ref[:, cols].astype(F32) + other_ref[:, cols].astype(F32))
            mine = (row >= begin[j]) & (row < end[j])
            outs[kv][...] = jnp.where(mine, grown, outs[kv][...].astype(F32)).astype(BF16)


def grow_call(facts, slot, shrunk, ups, own, other):
    rows, cols = shrunk.shape
    feat = ups.shape[3]
    by_tile = lambda i, *_: (i, 0)
    return pl.pallas_call(
        grow_kernel,
        grid_spec=pltpu.PrefetchScalarGridSpec(
            num_scalar_prefetch=5,
            grid=(rows // TILE,),
            in_specs=[
                pl.BlockSpec((TILE, cols), by_tile),
                pl.BlockSpec(ups.shape, lambda i, *_: (0, 0, 0, 0), pipeline_mode=pl.Buffered(1)),
                pl.BlockSpec((TILE, 2 * feat), by_tile),
                pl.BlockSpec((TILE, 2 * feat), by_tile),
            ],
            out_specs=[pl.BlockSpec((TILE, feat), by_tile)] * 2,
        ),
        out_shape=[jax.ShapeDtypeStruct((rows, feat), BF16)] * 2,
        compiler_params=pltpu.CompilerParams(
            dimension_semantics=("arbitrary",), vmem_limit_bytes=24 * 2**20
        ),
        cost_estimate=pl.CostEstimate(
            flops=4 * rows * cols * feat, bytes_accessed=6 * rows * feat * 2, transcendentals=0
        ),
    )(*facts[:4], slot, shrunk, ups, own, other)


def per_device(
    replicas,
    cores,
    hidden_states,
    kv_weight,
    pool_down,
    pool_up,
    adapter_rank,
    pool_row,
    request_adapter,
    request_length,
):
    rows, width = hidden_states.shape
    kv_cols = kv_weight.shape[2]
    held, rank_max = pool_down.shape[0], pool_down.shape[3]
    team = 4 if replicas % 4 == 0 else 1
    part = width // team
    me = lax.axis_index("replica")
    core = lax.axis_index("tensor")

    def other_core(x):
        return lax.ppermute(x, "tensor", [(0, 1), (1, 0)])

    wanted = table_lookup(request_adapter[0], pool_row)
    count = request_length.shape[1]
    table = jnp.concatenate([wanted, request_length[0]])[None]
    table = lax.all_to_all(jnp.tile(table, (replicas, 1)), "replica", 0, 0, tiled=True)
    place = jnp.arange(pool_row.shape[0], dtype=jnp.int32)
    row_rank = jnp.sum(jnp.where(pool_row[None, :] == place[:, None], adapter_rank[None, :], 0), axis=1)

    def facts(o):
        line = lax.dynamic_slice_in_dim(table, me ^ o, 1, 0)[0]
        return line[:count], line[count:]

    teams = replicas // team

    def swap(x, o):
        return lax.ppermute(x, "replica", [(i, i ^ o) for i in range(replicas)])

    def share(o):
        return lax.dynamic_slice_in_dim(hidden_states, ((me ^ o) % team) * part, part, 1)

    sent = [share(o) for o in range(1, team)]
    pool_down, *sent = lax.optimization_barrier((pool_down, *sent))
    tokens = [share(0)] + [swap(x, o + 1) for o, x in enumerate(sent)]
    downs = pool_down.reshape(held, width, 2 * rank_max)
    downs = jnp.concatenate([downs[:, i * part : (i + 1) * part] for i in range(team)] * teams, axis=0)
    downs, table = lax.optimization_barrier((downs, table))
    down_all = lax.all_to_all(
        downs,
        "replica",
        0,
        0,
        tiled=True,
    )

    product = jnp.dot(
        hidden_states, kv_weight.reshape(width, 2 * kv_cols), preferred_element_type=F32
    ).astype(BF16)
    feat = kv_cols // cores
    if cores == 2:

        def features(c):
            return jnp.concatenate(
                [lax.dynamic_slice_in_dim(product, kv * kv_cols + c * feat, feat, 1) for kv in range(2)], axis=1
            )

        base_own = features(core)
        base_other = other_core(features(1 - core))
    else:
        base_own = jnp.concatenate(
            [
                lax.psum_scatter(
                    product[:, kv * kv_cols : (kv + 1) * kv_cols], "tensor", scatter_dimension=1, tiled=True
                )
                for kv in range(2)
            ],
            axis=1,
        )
        base_other = jnp.zeros_like(base_own)

    all_need = table[:, :count]
    asked = jnp.sum(jnp.where(all_need // held == me, all_need % held, 0), axis=1)
    down_all, base_own, base_other, pool_up = lax.optimization_barrier(
        (down_all, base_own, base_other, pool_up)
    )
    ups = lax.all_to_all(
        jnp.concatenate([lax.dynamic_slice_in_dim(pool_up, asked[i], 1, 0) for i in range(replicas)], axis=0),
        "replica",
        0,
        0,
        tiled=True,
    )

    plans, needs = [], []
    for o in range(team):
        need, lengths = facts(o)
        needs.append(need)
        plans.append(plan(lengths, table_lookup(need, row_rank), rows))
    partial = shrink_call(
        [jnp.stack(f) for f in zip(*plans)], jnp.stack(needs), jnp.concatenate(tokens, axis=0), down_all
    ).reshape(team, rows, 2 * rank_max)
    if cores == 2:
        keep = lax.dynamic_slice_in_dim(partial, core * rank_max, rank_max, 2)
        give = lax.dynamic_slice_in_dim(partial, (1 - core) * rank_max, rank_max, 2)
        partial = (keep.astype(F32) + other_core(give).astype(F32)).astype(BF16)
    else:
        partial = lax.psum(partial, "tensor")
    total = partial[0].astype(F32)
    for o in range(1, team):
        total = total + swap(partial[o], o).astype(F32)
    shrunk = total.astype(BF16)
    if cores == 2:
        peer = other_core(shrunk)
        shrunk = jnp.concatenate(
            [jnp.where(core == 0, shrunk, peer), jnp.where(core == 0, peer, shrunk)], axis=1
        )

    keys, values = grow_call(plans[0], needs[0] // held, shrunk, ups, base_own, base_other)
    return keys, values


def solution(mesh):
    placed = (
        P(("groups", "replica"), "tensor"),
        P("tensor", None, None),
        P(("groups", "replica"), "tensor", None, None),
        P(("groups", "replica"), None, None, "tensor"),
        P("groups"),
        P("groups"),
        P(("groups", "replica"), None),
        P(("groups", "replica"), None),
    )
    return jax.shard_map(
        functools.partial(per_device, mesh.shape["replica"], mesh.shape["tensor"]),
        mesh=mesh,
        in_specs=placed,
        out_specs=(P(("groups", "replica"), "tensor"), P(("groups", "replica"), "tensor")),
        check_vma=False,
    )
```

```python
import functools

import jax
import jax.numpy as jnp
from jax import lax
from jax.experimental import pallas as pl
from jax.experimental.pallas import tpu as pltpu
from jax.sharding import PartitionSpec as P

TILE = 256
LOTS = 2
BF16 = jnp.bfloat16
F32 = jnp.float32


def table_lookup(indices, table):
    hit = indices[:, None] == jnp.arange(table.shape[0], dtype=jnp.int32)[None, :]
    return jnp.sum(jnp.where(hit, table[None, :], 0), axis=1)


def plan(lengths, ranks, rows):
    ends = jnp.cumsum(lengths)
    starts = ends - lengths
    top = jnp.arange(rows // TILE, dtype=jnp.int32) * TILE
    low = jnp.sum((ends[None, :] <= top[:, None]).astype(jnp.int32), axis=1)
    high = jnp.sum((starts[None, :] < top[:, None] + TILE).astype(jnp.int32), axis=1)
    return low, high, starts, ends, ranks, 1.0 / jnp.sqrt(ranks.astype(F32))


def shrink_kernel(first, low, high, begin, end, rank, scale, slot, column, h_ref, d_hbm, o_ref, d_ref, sems):
    g = pl.program_id(0)
    t = first + g
    top = t * TILE
    shape = o_ref.shape
    half = shape[1] // 2
    o_ref[...] = jnp.zeros(shape, o_ref.dtype)

    def fetch(j):
        return pltpu.make_async_copy(d_hbm.at[slot[j]], d_ref.at[j], sems.at[j])

    @pl.when(g == 0)
    def _():
        @pl.loop(low[first], high[first + pl.num_programs(0) - 1])
        def _(j):
            fetch(j).start()

    @pl.loop(low[t], high[t])
    def _(j):
        @pl.when((g == 0) | (begin[j] >= top))
        def _():
            fetch(j).wait()

        grown = jnp.dot(h_ref[...], d_ref[j], preferred_element_type=F32) * scale[j]
        row = lax.broadcasted_iota(jnp.int32, shape, 0) + top
        col = lax.broadcasted_iota(jnp.int32, shape, 1)
        col = jnp.where(col >= half, col - half, col)
        mine = (row >= begin[j]) & (row < end[j])
        value = jnp.where(col < rank[j], grown, 0.0)
        o_ref[...] = jnp.where(mine, value, o_ref[...].astype(F32)).astype(o_ref.dtype)


def shrink_call(facts, slot, first, tokens, column, downs):
    _, width, cols = downs.shape
    rows = tokens.shape[0]
    tiles = rows // TILE
    count = slot.shape[0]
    return pl.pallas_call(
        functools.partial(shrink_kernel, first),
        grid_spec=pltpu.PrefetchScalarGridSpec(
            num_scalar_prefetch=8,
            grid=(tiles,),
            in_specs=[
                pl.BlockSpec((TILE, width), lambda i, *refs: (i, refs[7][0])),
                pl.BlockSpec(memory_space=pl.ANY),
            ],
            out_specs=pl.BlockSpec((TILE, cols), lambda i, *_: (i, 0)),
            scratch_shapes=[
                pltpu.VMEM((count, width, cols), BF16),
                pltpu.SemaphoreType.DMA((count,)),
            ],
        ),
        out_shape=jax.ShapeDtypeStruct((rows, cols), BF16),
        compiler_params=pltpu.CompilerParams(
            dimension_semantics=("arbitrary",), vmem_limit_bytes=16 * 2**20
        ),
        cost_estimate=pl.CostEstimate(
            flops=4 * rows * width * cols, bytes_accessed=2 * rows * width * 2, transcendentals=0
        ),
    )(*facts, slot, column, tokens, downs)


def grow_kernel(first, low, high, begin, end, slot, s_ref, u_ref, own_ref, other_ref, *refs):
    k_ref, v_ref, wide = refs[-3:]
    t = first + pl.program_id(0)
    half = s_ref.shape[1] // 2
    outs = (k_ref, v_ref)
    feat = k_ref.shape[1]
    row = lax.broadcasted_iota(jnp.int32, (TILE, half), 0) + t * TILE
    wide[...] = jnp.zeros(wide.shape, BF16)

    @pl.loop(low[t], high[t])
    def _(j):
        mine = (row >= begin[j]) & (row < end[j])
        for kv in range(2):
            part = s_ref[:, kv * half : (kv + 1) * half].astype(F32)
            wide[kv, :, pl.ds(pl.multiple_of(slot[j] * half, half), half)] = jnp.where(mine, part, 0.0).astype(BF16)

    for kv in range(2):
        cols = slice(kv * feat, (kv + 1) * feat)
        ups = u_ref[:, kv].reshape(-1, feat)
        grown = jnp.dot(wide[kv], ups, preferred_element_type=F32)
        grown = grown + (own_ref[:, cols].astype(F32) + other_ref[:, cols].astype(F32))
        outs[kv][...] = grown.astype(BF16)


def grow_call(facts, slot, first, shrunk, ups, own, other, before):
    rows, cols = shrunk.shape
    feat = ups.shape[3]
    by_tile = lambda i, *_: (first + i, 0)
    return pl.pallas_call(
        functools.partial(grow_kernel, first),
        grid_spec=pltpu.PrefetchScalarGridSpec(
            num_scalar_prefetch=5,
            grid=(rows // TILE,),
            in_specs=[
                pl.BlockSpec((TILE, cols), lambda i, *_: (i, 0)),
                pl.BlockSpec(ups.shape, lambda i, *_: (0, 0, 0, 0), pipeline_mode=pl.Buffered(1)),
                pl.BlockSpec((TILE, 2 * feat), by_tile),
                pl.BlockSpec((TILE, 2 * feat), by_tile),
            ]
            + [pl.BlockSpec(memory_space=pl.ANY)] * len(before),
            out_specs=[pl.BlockSpec((TILE, feat), by_tile)] * 2,
            scratch_shapes=[pltpu.VMEM((2, TILE, ups.shape[0] * cols // 2), BF16)],
        ),
        out_shape=[jax.ShapeDtypeStruct((own.shape[0], feat), BF16)] * 2,
        input_output_aliases={9 + i: i for i in range(len(before))},
        compiler_params=pltpu.CompilerParams(
            dimension_semantics=("arbitrary",), vmem_limit_bytes=16 * 2**20
        ),
        cost_estimate=pl.CostEstimate(
            flops=4 * rows * cols * feat, bytes_accessed=6 * rows * feat * 2, transcendentals=0
        ),
    )(*facts[:4], slot, shrunk, ups, own, other, *before)


def send_kernel(pool_ref, o_ref):
    for t in range(o_ref.shape[0]):
        o_ref[t, 0, 0] = pool_ref[0]


def send_call(team, teams, pool_down):
    held, width, kinds, rank = pool_down.shape
    part = width // team
    return pl.pallas_call(
        send_kernel,
        grid=(team, held),
        in_specs=[pl.BlockSpec((1, part, kinds, rank), lambda i, a: (a, i, 0, 0))],
        out_specs=pl.BlockSpec((teams, 1, 1, part, kinds, rank), lambda i, a: (0, i, a, 0, 0, 0)),
        out_shape=jax.ShapeDtypeStruct((teams, team, held, part, kinds, rank), BF16),
        compiler_params=pltpu.CompilerParams(vmem_limit_bytes=32 * 2**20),
    )(pool_down).reshape(-1, part, kinds, rank)


def per_device(
    replicas,
    cores,
    hidden_states,
    kv_weight,
    pool_down,
    pool_up,
    adapter_rank,
    pool_row,
    request_adapter,
    request_length,
):
    rows, width = hidden_states.shape
    kv_cols = kv_weight.shape[2]
    held, rank_max = pool_down.shape[0], pool_down.shape[3]
    team = 4 if replicas % 4 == 0 else 1
    part = width // team
    me = lax.axis_index("replica")
    core = lax.axis_index("tensor")

    def other_core(x):
        return lax.ppermute(x, "tensor", [(0, 1), (1, 0)])

    wanted = table_lookup(request_adapter[0], pool_row)
    count = request_length.shape[1]
    table = jnp.concatenate([wanted, request_length[0]])[None]
    table = lax.all_to_all(jnp.tile(table, (replicas, 1)), "replica", 0, 0, tiled=True)
    place = jnp.arange(pool_row.shape[0], dtype=jnp.int32)
    row_rank = jnp.sum(jnp.where(pool_row[None, :] == place[:, None], adapter_rank[None, :], 0), axis=1)

    def facts(o):
        line = lax.dynamic_slice_in_dim(table, me ^ o, 1, 0)[0]
        return line[:count], line[count:]

    teams = replicas // team

    def swap(x, o):
        return lax.ppermute(x, "replica", [(i, i ^ o) for i in range(replicas)])

    lot = rows // LOTS

    def share(o, c):
        cut = lax.dynamic_slice(hidden_states, (c * lot, ((me ^ o) % team) * part), (lot, part))
        return swap(cut, o)

    early = [share(o, 0) for o in range(1, team)]
    downs = send_call(team, teams, pool_down)
    downs, table = lax.optimization_barrier((downs, table))
    down_all = lax.all_to_all(
        downs,
        "replica",
        0,
        0,
        tiled=True,
    )

    late = [[share(o, c) for o in range(1, team)] for c in range(1, LOTS)]

    product = jnp.dot(
        hidden_states, kv_weight.reshape(width, 2 * kv_cols), preferred_element_type=F32
    ).astype(BF16)
    feat = kv_cols // cores
    if cores == 2:

        def features(c):
            return jnp.concatenate(
                [lax.dynamic_slice_in_dim(product, kv * kv_cols + c * feat, feat, 1) for kv in range(2)], axis=1
            )

        base_own = features(core)
        base_other = other_core(features(1 - core))
    else:
        base_own = jnp.concatenate(
            [
                lax.psum_scatter(
                    product[:, kv * kv_cols : (kv + 1) * kv_cols], "tensor", scatter_dimension=1, tiled=True
                )
                for kv in range(2)
            ],
            axis=1,
        )
        base_other = jnp.zeros_like(base_own)

    all_need = table[:, :count]
    asked = jnp.sum(jnp.where(all_need // held == me, all_need % held, 0), axis=1)
    down_all, pool_up = lax.optimization_barrier((down_all, pool_up))
    early, base_own, base_other = lax.optimization_barrier((early, base_own, base_other))
    tokens = [early] + late
    down_all = down_all.reshape(-1, part, 2 * rank_max)
    ups = lax.all_to_all(
        jnp.concatenate([lax.dynamic_slice_in_dim(pool_up, asked[i], 1, 0) for i in range(replicas)], axis=0),
        "replica",
        0,
        0,
        tiled=True,
    )

    plans, needs = [], []
    for o in range(team):
        need, lengths = facts(o)
        needs.append(need)
        plans.append(plan(lengths, table_lookup(need, row_rank), rows))
    column = jnp.reshape(me % team, (1,)).astype(jnp.int32)
    zero = jnp.zeros((1,), jnp.int32)

    def over_cores(one):
        if cores != 2:
            return lax.psum(one, "tensor")
        keep = lax.dynamic_slice_in_dim(one, core * rank_max, rank_max, 1)
        give = lax.dynamic_slice_in_dim(one, (1 - core) * rank_max, rank_max, 1)
        return (keep.astype(F32) + other_core(give).astype(F32)).astype(BF16)

    own = over_cores(shrink_call(plans[0], needs[0], 0, hidden_states, column, down_all))
    out = ()
    per_lot = lot // TILE
    for c in range(LOTS):
        total = own[c * lot : (c + 1) * lot].astype(F32)
        for o in range(1, team):
            one = over_cores(shrink_call(plans[o], needs[o], c * per_lot, tokens[c][o - 1], zero, down_all))
            total = total + swap(one, o).astype(F32)
        shrunk = total.astype(BF16)
        if cores == 2:
            peer = other_core(shrunk)
            shrunk = jnp.concatenate(
                [jnp.where(core == 0, shrunk, peer), jnp.where(core == 0, peer, shrunk)], axis=1
            )
        out = grow_call(plans[0], needs[0] // held, c * per_lot, shrunk, ups, base_own, base_other, out)
    keys, values = out
    return keys, values


def solution(mesh):
    placed = (
        P(("groups", "replica"), "tensor"),
        P("tensor", None, None),
        P(("groups", "replica"), "tensor", None, None),
        P(("groups", "replica"), None, None, "tensor"),
        P("groups"),
        P("groups"),
        P(("groups", "replica"), None),
        P(("groups", "replica"), None),
    )
    return jax.shard_map(
        functools.partial(per_device, mesh.shape["replica"], mesh.shape["tensor"]),
        mesh=mesh,
        in_specs=placed,
        out_specs=(P(("groups", "replica"), "tensor"), P(("groups", "replica"), "tensor")),
        check_vma=False,
    )
```

```python
import functools

import jax
import jax.numpy as jnp
from jax import lax
from jax.experimental import pallas as pl
from jax.experimental.pallas import tpu as pltpu
from jax.sharding import PartitionSpec as P

TILE = 256
LOTS = 2
BF16 = jnp.bfloat16
F32 = jnp.float32


def table_lookup(indices, table):
    hit = indices[:, None] == jnp.arange(table.shape[0], dtype=jnp.int32)[None, :]
    return jnp.sum(jnp.where(hit, table[None, :], 0), axis=1)


def plan(lengths, ranks, rows):
    ends = jnp.cumsum(lengths)
    starts = ends - lengths
    top = jnp.arange(rows // TILE, dtype=jnp.int32) * TILE
    low = jnp.sum((ends[None, :] <= top[:, None]).astype(jnp.int32), axis=1)
    high = jnp.sum((starts[None, :] < top[:, None] + TILE).astype(jnp.int32), axis=1)
    return low, high, starts, ends, ranks, 1.0 / jnp.sqrt(ranks.astype(F32))


def shrink_kernel(first, low, high, begin, end, rank, scale, slot, column, h_ref, d_hbm, o_ref, d_ref, sems):
    g = pl.program_id(0)
    t = first + g
    top = t * TILE
    shape = o_ref.shape
    half = shape[1] // 2
    o_ref[...] = jnp.zeros(shape, o_ref.dtype)

    def fetch(j):
        return pltpu.make_async_copy(d_hbm.at[slot[j]], d_ref.at[j], sems.at[j])

    @pl.when(g == 0)
    def _():
        @pl.loop(low[first], high[first + pl.num_programs(0) - 1])
        def _(j):
            fetch(j).start()

    @pl.loop(low[t], high[t])
    def _(j):
        @pl.when((g == 0) | (begin[j] >= top))
        def _():
            fetch(j).wait()

        grown = jnp.dot(h_ref[...], d_ref[j], preferred_element_type=F32) * scale[j]
        row = lax.broadcasted_iota(jnp.int32, shape, 0) + top
        col = lax.broadcasted_iota(jnp.int32, shape, 1)
        col = jnp.where(col >= half, col - half, col)
        mine = (row >= begin[j]) & (row < end[j])
        value = jnp.where(col < rank[j], grown, 0.0)
        o_ref[...] = jnp.where(mine, value, o_ref[...].astype(F32)).astype(o_ref.dtype)


def shrink_call(facts, slot, first, tokens, column, downs):
    _, width, cols = downs.shape
    rows = tokens.shape[0]
    tiles = rows // TILE
    count = slot.shape[0]
    return pl.pallas_call(
        functools.partial(shrink_kernel, first),
        grid_spec=pltpu.PrefetchScalarGridSpec(
            num_scalar_prefetch=8,
            grid=(tiles,),
            in_specs=[
                pl.BlockSpec((TILE, width), lambda i, *refs: (i, refs[7][0])),
                pl.BlockSpec(memory_space=pl.ANY),
            ],
            out_specs=pl.BlockSpec((TILE, cols), lambda i, *_: (i, 0)),
            scratch_shapes=[
                pltpu.VMEM((count, width, cols), BF16),
                pltpu.SemaphoreType.DMA((count,)),
            ],
        ),
        out_shape=jax.ShapeDtypeStruct((rows, cols), BF16),
        compiler_params=pltpu.CompilerParams(
            dimension_semantics=("arbitrary",), vmem_limit_bytes=16 * 2**20
        ),
        cost_estimate=pl.CostEstimate(
            flops=4 * rows * width * cols, bytes_accessed=2 * rows * width * 2, transcendentals=0
        ),
    )(*facts, slot, column, tokens, downs)


def grow_kernel(first, low, high, begin, end, slot, s_ref, u_ref, own_ref, other_ref, *refs):
    k_ref, v_ref, wide = refs[-3:]
    t = first + pl.program_id(0)
    half = s_ref.shape[1] // 2
    outs = (k_ref, v_ref)
    feat = k_ref.shape[1]
    row = lax.broadcasted_iota(jnp.int32, (TILE, half), 0) + t * TILE
    wide[...] = jnp.zeros(wide.shape, BF16)

    @pl.loop(low[t], high[t])
    def _(j):
        mine = (row >= begin[j]) & (row < end[j])
        for kv in range(2):
            part = s_ref[:, kv * half : (kv + 1) * half].astype(F32)
            wide[kv, :, pl.ds(pl.multiple_of(slot[j] * half, half), half)] = jnp.where(mine, part, 0.0).astype(BF16)

    for kv in range(2):
        cols = slice(kv * feat, (kv + 1) * feat)
        ups = u_ref[:, kv].reshape(-1, feat)
        grown = jnp.dot(wide[kv], ups, preferred_element_type=F32)
        grown = grown + (own_ref[:, cols].astype(F32) + other_ref[:, cols].astype(F32))
        outs[kv][...] = grown.astype(BF16)


def grow_call(facts, slot, first, shrunk, ups, own, other, before):
    rows, cols = shrunk.shape
    feat = ups.shape[3]
    by_tile = lambda i, *_: (first + i, 0)
    return pl.pallas_call(
        functools.partial(grow_kernel, first),
        grid_spec=pltpu.PrefetchScalarGridSpec(
            num_scalar_prefetch=5,
            grid=(rows // TILE,),
            in_specs=[
                pl.BlockSpec((TILE, cols), lambda i, *_: (i, 0)),
                pl.BlockSpec(ups.shape, lambda i, *_: (0, 0, 0, 0), pipeline_mode=pl.Buffered(1)),
                pl.BlockSpec((TILE, 2 * feat), by_tile),
                pl.BlockSpec((TILE, 2 * feat), by_tile),
            ]
            + [pl.BlockSpec(memory_space=pl.ANY)] * len(before),
            out_specs=[pl.BlockSpec((TILE, feat), by_tile)] * 2,
            scratch_shapes=[pltpu.VMEM((2, TILE, ups.shape[0] * cols // 2), BF16)],
        ),
        out_shape=[jax.ShapeDtypeStruct((own.shape[0], feat), BF16)] * 2,
        input_output_aliases={9 + i: i for i in range(len(before))},
        compiler_params=pltpu.CompilerParams(
            dimension_semantics=("arbitrary",), vmem_limit_bytes=16 * 2**20
        ),
        cost_estimate=pl.CostEstimate(
            flops=4 * rows * cols * feat, bytes_accessed=6 * rows * feat * 2, transcendentals=0
        ),
    )(*facts[:4], slot, shrunk, ups, own, other, *before)


def send_kernel(pool_ref, o_ref):
    for t in range(o_ref.shape[0]):
        o_ref[t, 0, 0] = pool_ref[0]


def send_call(team, teams, pool_down):
    held, width, kinds, rank = pool_down.shape
    part = width // team
    return pl.pallas_call(
        send_kernel,
        grid=(team, held),
        in_specs=[pl.BlockSpec((1, part, kinds, rank), lambda i, a: (a, i, 0, 0))],
        out_specs=pl.BlockSpec((teams, 1, 1, part, kinds, rank), lambda i, a: (0, i, a, 0, 0, 0)),
        out_shape=jax.ShapeDtypeStruct((teams, team, held, part, kinds, rank), BF16),
        compiler_params=pltpu.CompilerParams(vmem_limit_bytes=32 * 2**20),
    )(pool_down).reshape(-1, part, kinds, rank)


def per_device(
    replicas,
    cores,
    hidden_states,
    kv_weight,
    pool_down,
    pool_up,
    adapter_rank,
    pool_row,
    request_adapter,
    request_length,
):
    rows, width = hidden_states.shape
    kv_cols = kv_weight.shape[2]
    held, rank_max = pool_down.shape[0], pool_down.shape[3]
    team = 4 if replicas % 4 == 0 else 1
    part = width // team
    me = lax.axis_index("replica")
    core = lax.axis_index("tensor")

    def other_core(x):
        return lax.ppermute(x, "tensor", [(0, 1), (1, 0)])

    wanted = table_lookup(request_adapter[0], pool_row)
    count = request_length.shape[1]
    table = jnp.concatenate([wanted, request_length[0]])[None]
    table = lax.all_to_all(jnp.tile(table, (replicas, 1)), "replica", 0, 0, tiled=True)
    place = jnp.arange(pool_row.shape[0], dtype=jnp.int32)
    row_rank = jnp.sum(jnp.where(pool_row[None, :] == place[:, None], adapter_rank[None, :], 0), axis=1)

    def facts(o):
        line = lax.dynamic_slice_in_dim(table, me ^ o, 1, 0)[0]
        return line[:count], line[count:]

    teams = replicas // team

    def swap(x, o):
        return lax.ppermute(x, "replica", [(i, i ^ o) for i in range(replicas)])

    lot = rows // LOTS

    def share(hidden, o, c):
        cut = lax.dynamic_slice(hidden, (c * lot, ((me ^ o) % team) * part), (lot, part))
        return swap(cut, o)

    early = [share(hidden_states, o, 0) for o in range(1, team)]
    downs = send_call(team, teams, pool_down)
    downs, table = lax.optimization_barrier((downs, table))
    down_all = lax.all_to_all(
        downs,
        "replica",
        0,
        0,
        tiled=True,
    )

    early, hidden = lax.optimization_barrier((early, hidden_states))
    late = [[share(hidden, o, c) for o in range(1, team)] for c in range(1, LOTS)]

    product = jnp.dot(
        hidden_states, kv_weight.reshape(width, 2 * kv_cols), preferred_element_type=F32
    ).astype(BF16)
    feat = kv_cols // cores
    if cores == 2:

        def features(c):
            return jnp.concatenate(
                [lax.dynamic_slice_in_dim(product, kv * kv_cols + c * feat, feat, 1) for kv in range(2)], axis=1
            )

        base_own = features(core)
        base_other = other_core(features(1 - core))
    else:
        base_own = jnp.concatenate(
            [
                lax.psum_scatter(
                    product[:, kv * kv_cols : (kv + 1) * kv_cols], "tensor", scatter_dimension=1, tiled=True
                )
                for kv in range(2)
            ],
            axis=1,
        )
        base_other = jnp.zeros_like(base_own)

    all_need = table[:, :count]
    asked = jnp.sum(jnp.where(all_need // held == me, all_need % held, 0), axis=1)
    down_all, pool_up = lax.optimization_barrier((down_all, pool_up))
    early, base_own, base_other = lax.optimization_barrier((early, base_own, base_other))
    tokens = [early] + late
    down_all = down_all.reshape(-1, part, 2 * rank_max)
    ups = lax.all_to_all(
        jnp.concatenate([lax.dynamic_slice_in_dim(pool_up, asked[i], 1, 0) for i in range(replicas)], axis=0),
        "replica",
        0,
        0,
        tiled=True,
    )

    plans, needs = [], []
    for o in range(team):
        need, lengths = facts(o)
        needs.append(need)
        plans.append(plan(lengths, table_lookup(need, row_rank), rows))
    column = jnp.reshape(me % team, (1,)).astype(jnp.int32)
    zero = jnp.zeros((1,), jnp.int32)

    def over_cores(one):
        if cores != 2:
            return lax.psum(one, "tensor")
        keep = lax.dynamic_slice_in_dim(one, core * rank_max, rank_max, 1)
        give = lax.dynamic_slice_in_dim(one, (1 - core) * rank_max, rank_max, 1)
        return (keep.astype(F32) + other_core(give).astype(F32)).astype(BF16)

    own = over_cores(shrink_call(plans[0], needs[0], 0, hidden_states, column, down_all))
    shrunk = []
    per_lot = lot // TILE
    for c in range(LOTS):
        one = {0: own[c * lot : (c + 1) * lot]}
        for o in range(1, team):
            one[o] = over_cores(shrink_call(plans[o], needs[o], c * per_lot, tokens[c][o - 1], zero, down_all))
        step = 1
        while step < team:
            got = {o: swap(one[o + step], step) for o in range(0, team, 2 * step)}
            one = {o: (one[o].astype(F32) + x.astype(F32)).astype(BF16) for o, x in got.items()}
            step *= 2
        shrunk.append(one[0])
    shrunk = jnp.concatenate(shrunk, axis=0)
    if cores == 2:
        peer = other_core(shrunk)
        shrunk = jnp.concatenate([jnp.where(core == 0, shrunk, peer), jnp.where(core == 0, peer, shrunk)], axis=1)
    keys, values = grow_call(plans[0], needs[0] // held, 0, shrunk, ups, base_own, base_other, ())
    return keys, values


def solution(mesh):
    placed = (
        P(("groups", "replica"), "tensor"),
        P("tensor", None, None),
        P(("groups", "replica"), "tensor", None, None),
        P(("groups", "replica"), None, None, "tensor"),
        P("groups"),
        P("groups"),
        P(("groups", "replica"), None),
        P(("groups", "replica"), None),
    )
    return jax.shard_map(
        functools.partial(per_device, mesh.shape["replica"], mesh.shape["tensor"]),
        mesh=mesh,
        in_specs=placed,
        out_specs=(P(("groups", "replica"), "tensor"), P(("groups", "replica"), "tensor")),
        check_vma=False,
    )
```
